256 devices in a mesh: ctx: 32 (over y, z), tp: 8 (over x, core).
Axes of the slice: x: 4, y: 4, z: 8, core: 2. Of those that a mesh axis runs over, the one named last changes fastest.
Arguments:
- queries: bfloat16 [16384, 8192], P('ctx', 'tp'), may hold values from -6 to 6
- keys: bfloat16 [16384, 8192], P('ctx', 'tp'), may hold values from -6 to 6
- values: bfloat16 [16384, 8192], P('ctx', 'tp'), may hold values from -75 to 75
- gate: bfloat16 [16384, 8192], P('ctx', 'tp'), may hold values from -6 to 6
- gain: float32 [8192], P('tp'), may hold values from 0.1 to 1.9
- out_grad: bfloat16 [16384, 8192], P('ctx', 'tp'), may hold values from -6 to 6
Outputs:
- output: bfloat16 [16384, 8192], P('ctx', 'tp')
- query_grad: bfloat16 [16384, 8192], P('ctx', 'tp')
- key_grad: bfloat16 [16384, 8192], P('ctx', 'tp')
- value_grad: bfloat16 [16384, 8192], P('ctx', 'tp')
- gate_grad: bfloat16 [16384, 8192], P('ctx', 'tp')
The draws below stay inside these ranges and needn't reach their ends.
All inputs are finite; a program needn't handle non-finite values.
Results may differ from the reference program's by a relative error of at most 0.005.
Values sent between devices are 32-bit elements; how exact they have to be, the bound alone decides.
No kernel may reach another device: no remote copies, remote signals or barrier semaphores. Data moves between devices by JAX's collectives and lax.ppermute only.
A program may use at most 128 MiB of HBM per device.

```python
import math
import jax
import jax.numpy as jnp
from jax import lax

HEADS = 64
HD = 128
BLOCK = 512
D = 8192
SEQ = 16384


def draw_values(key, part):
    key = jax.random.fold_in(key, 7)
    base_key, jitter_key = jax.random.split(key)
    column = jnp.arange(D, dtype=jnp.float32) / D
    jitter = jnp.exp(jax.random.uniform(jitter_key, (D,), jnp.float32, -0.2, 0.2))
    ramp = jnp.exp(math.log(10.0) * column)
    base = jnp.clip(jax.random.normal(base_key, (SEQ, D), jnp.float32), -6.0, 6.0)
    return (base * (ramp * jitter)[None, :]).astype(jnp.bfloat16)


def levels(own_key, shape, cuts, smallest, largest):
    factor_of = 1.0
    for dim, shards_of in cuts:
        steps = jax.random.uniform(jax.random.fold_in(jax.random.fold_in(own_key, 6), dim), (shards_of,), jnp.float32, smallest / len(cuts), largest / len(cuts))
        factor_of = factor_of * jnp.repeat(jnp.exp(steps), shape[dim] // shards_of).reshape((-1,) + (1,) * (len(shape) - 1 - dim))
    return factor_of


def bell_draw(stream_key, extent, scale, reach, cuts=(), kind=jnp.bfloat16):
    level = levels(stream_key, extent, cuts, -0.22, 0.18) if cuts else 1.0
    result = jax.random.normal(stream_key, extent, jnp.float32) * scale * level
    return jnp.minimum(jnp.maximum(result, -reach), reach).astype(kind)


def setup_inputs(seed: int = 0) -> dict:
    seeds = jax.random.split(jax.random.key(seed), 7)
    return {
        "queries": bell_draw(seeds[0], (SEQ, D), 1.0, 6.0, ((0, 32), (1, 8))),
        "keys": bell_draw(seeds[1], (SEQ, D), 1.0, 6.0, ((0, 32), (1, 8))),
        "values": draw_values(jax.random.fold_in(seeds[6], 71), 0),
        "gate": bell_draw(seeds[3], (SEQ, D), 1.0, 6.0, ((0, 32), (1, 8))),
        "gain": jnp.clip(1.0 + 0.18 * jax.random.normal(seeds[4], (D,), jnp.float32), 0.1, 1.9),
        "out_grad": bell_draw(seeds[5], (SEQ, D), 1.0, 6.0, ((0, 32), (1, 8))),
    }


EPS = 1e-06

def blocks(x):
    return x.reshape(SEQ // BLOCK, BLOCK, HD).astype(jnp.float32)

def causal():
    rows = jnp.arange(BLOCK)[:, None]
    cols = jnp.arange(BLOCK)[None, :]
    return cols <= rows

def rounded(x):
    narrow = lax.optimization_barrier(x.astype(jnp.bfloat16))
    return narrow.astype(jnp.float32)

def head_parts(q_head, k_head, v_head):
    q_full, k_full, v_full = (blocks(q_head), blocks(k_head), blocks(v_head))
    attn = rounded(jnp.where(causal(), jnp.einsum('nbe,nce->nbc', q_full, k_full), 0.0))
    block_kv = jnp.einsum('nce,ncf->nef', k_full, v_full)
    states = jnp.cumsum(block_kv, 0) - block_kv
    return (q_full, k_full, v_full, attn, states)

def forward_head(items):
    q_full, k_full, v_full, attn, states = head_parts(*items)
    mixed = jnp.einsum('nbc,ncf->nbf', attn, v_full) + jnp.einsum('nbe,nef->nbf', q_full, states, precision=lax.Precision.HIGHEST)
    return mixed.reshape(SEQ, HD)

def backward_head(items):
    q_full, k_full, v_full, attn, states = head_parts(items[0], items[1], items[2])
    d_full = blocks(items[3])
    prob = rounded(jnp.where(causal(), jnp.einsum('nbf,ncf->nbc', d_full, v_full), 0.0))
    high = lax.Precision.HIGHEST
    q_grad = jnp.einsum('nbc,nce->nbe', prob, k_full) + jnp.einsum('nbf,nef->nbe', d_full, states, precision=high)
    block_g = jnp.einsum('nbe,nbf->nef', q_full, d_full)
    after = jnp.flip(jnp.cumsum(jnp.flip(block_g, 0), 0), 0) - block_g
    k_grad = jnp.einsum('nbc,nbe->nce', prob, q_full) + jnp.einsum('ncf,nef->nce', v_full, after, precision=high)
    v_grad = jnp.einsum('nbc,nbf->ncf', attn, d_full) + jnp.einsum('nce,nef->ncf', k_full, after, precision=high)
    return (q_grad.reshape(SEQ, HD).astype(jnp.bfloat16), k_grad.reshape(SEQ, HD).astype(jnp.bfloat16), v_grad.reshape(SEQ, HD).astype(jnp.bfloat16))

def by_head(x):
    return x.reshape(SEQ, HEADS, HD).transpose(1, 0, 2)

def unhead(x):
    return x.transpose(1, 0, 2).reshape(SEQ, D)

def reference(queries, keys, values, gate, gain, out_grad):
    mixed = unhead(lax.map(forward_head, (by_head(queries), by_head(keys), by_head(values))))
    sig = jax.nn.sigmoid(gate.astype(jnp.float32))
    inv_rms = lax.rsqrt(lax.optimization_barrier(jnp.mean(mixed * mixed, axis=1, keepdims=True)) + EPS)
    normed = mixed * inv_rms
    output = (normed * gain * sig).astype(jnp.bfloat16)
    dy_full = out_grad.astype(jnp.float32)
    dn = dy_full * gain * sig
    project = lax.optimization_barrier(jnp.mean(dn * normed, axis=1, keepdims=True))
    mixed_grad = (inv_rms * (dn - normed * project)).astype(jnp.bfloat16)
    gate_grad = (dy_full * gain * normed * sig * (1.0 - sig)).astype(jnp.bfloat16)
    q_grad, k_grad, v_grad = lax.map(backward_head, (by_head(queries), by_head(keys), by_head(values), by_head(mixed_grad)))
    return (output, unhead(q_grad), unhead(k_grad), unhead(v_grad), gate_grad)
```

```python
import jax
import jax.numpy as jnp
from jax import lax
from jax.experimental import pallas as pl
from jax.experimental.pallas import tpu as pltpu
from jax.sharding import PartitionSpec as P

HD = 128
D = 8192
EPS = 1e-06
HALF = 256
PAIR = 2 * HD
F32 = jnp.float32
BF16 = jnp.bfloat16


def dot(a, b, dims):
    return lax.dot_general(a, b, (dims, ((), ())), preferred_element_type=F32)


def nn(a, b):
    return dot(a, b, ((1,), (0,)))


def nt(a, b):
    return dot(a, b, ((1,), (1,)))


def tn(a, b):
    return dot(a, b, ((0,), (0,)))


def halves(x):
    high = x.astype(BF16)
    return high, (x - high.astype(F32)).astype(BF16)


def causal_tile(x):
    rows = lax.broadcasted_iota(jnp.int32, x.shape, 0)
    cols = lax.broadcasted_iota(jnp.int32, x.shape, 1)
    return jnp.where(cols <= rows, x, 0.0)


def state_kernel(k_ref, v_ref, out_ref):
    for h in range(2):
        cols = slice(h * HD, (h + 1) * HD)
        out_ref[cols, :] = tn(k_ref[:, cols], v_ref[:, cols])


def scan_kernel(reverse, x_ref, out_ref):
    count = x_ref.shape[0]
    running = jnp.zeros(x_ref.shape[1:], F32)
    for step in range(count):
        i = count - 1 - step if reverse else step
        out_ref[i] = running
        running = running + x_ref[i]


def forward_kernel(q_ref, k_ref, v_ref, s_ref, gate_ref, gain_ref, dy_ref,
                   mixed_ref, attn_ref, sums_ref, square, cross):
    step = pl.program_id(0)

    @pl.when(step == 0)
    def _():
        square[...] = jnp.zeros_like(square)
        cross[...] = jnp.zeros_like(cross)

    for h in range(2):
        cols = slice(h * HD, (h + 1) * HD)
        q, k, v = q_ref[:, cols], k_ref[:, cols], v_ref[:, cols]
        q0, q1 = q[:HALF], q[HALF:]
        a00 = causal_tile(nt(q0, k[:HALF])).astype(BF16)
        a10 = nt(q1, k[:HALF]).astype(BF16)
        a11 = causal_tile(nt(q1, k[HALF:])).astype(BF16)
        attn_ref[h, 0] = a00
        attn_ref[h, 1] = a10
        attn_ref[h, 2] = a11
        high, low = halves(s_ref[cols, :])
        stacked = jnp.concatenate([high, low], 0)
        inter = nn(jnp.concatenate([q, q], 1), stacked)
        intra0 = nn(a00, v[:HALF])
        intra1 = nn(a10, v[:HALF]) + nn(a11, v[HALF:])
        mixed = jnp.concatenate([intra0, intra1], 0) + inter
        mixed_ref[:, cols] = mixed
        sig = jax.nn.sigmoid(gate_ref[:, cols].astype(F32))
        dn = dy_ref[:, cols].astype(F32) * gain_ref[:, cols] * sig
        square[...] += mixed * mixed
        cross[...] += dn * mixed

    @pl.when(step == pl.num_programs(0) - 1)
    def _():
        sums_ref[0:1, :] = jnp.sum(square[...].T, axis=0, keepdims=True)
        sums_ref[1:2, :] = jnp.sum(cross[...].T, axis=0, keepdims=True)


def norm_kernel(sums_ref, mixed_ref, gate_ref, gain_ref, dy_ref, q_ref,
                out_ref, ggrad_ref, d_ref, g_ref, inv_ref, proj_ref):
    @pl.when(pl.program_id(0) == 0)
    def _():
        total = sums_ref[...]
        inv = lax.rsqrt(total[0:1] / D + EPS)
        proj = inv * (total[1:2] / D)
        inv_ref[...] = jnp.broadcast_to(inv, (HD, inv.shape[1])).T
        proj_ref[...] = jnp.broadcast_to(proj, (HD, proj.shape[1])).T

    for h in range(2):
        cols = slice(h * HD, (h + 1) * HD)
        inv, proj = inv_ref[...], proj_ref[...]
        sig = jax.nn.sigmoid(gate_ref[:, cols].astype(F32))
        dy_gain = dy_ref[:, cols].astype(F32) * gain_ref[:, cols]
        normed = mixed_ref[:, cols] * inv
        out_ref[:, cols] = (normed * gain_ref[:, cols] * sig).astype(BF16)
        dn = dy_gain * sig
        grad = (inv * (dn - normed * proj)).astype(BF16)
        ggrad_ref[:, cols] = (dy_gain * normed * sig * (1.0 - sig)).astype(BF16)
        d_ref[:, cols] = grad
        g_ref[cols, :] = tn(q_ref[:, cols], grad)


def backward_kernel(q_ref, k_ref, v_ref, d_ref, attn_ref, s_ref, after_ref,
                    qg_ref, kg_ref, vg_ref):
    for h in range(2):
        cols = slice(h * HD, (h + 1) * HD)
        q, k, v, d = q_ref[:, cols], k_ref[:, cols], v_ref[:, cols], d_ref[:, cols]
        d0, d1, q0, q1 = d[:HALF], d[HALF:], q[:HALF], q[HALF:]
        p00 = causal_tile(nt(d0, v[:HALF])).astype(BF16)
        p10 = nt(d1, v[:HALF]).astype(BF16)
        p11 = causal_tile(nt(d1, v[HALF:])).astype(BF16)
        a00, a10, a11 = attn_ref[h, 0], attn_ref[h, 1], attn_ref[h, 2]
        s_pair = jnp.concatenate(halves(s_ref[cols, :]), 1)
        after_high, after_low = halves(after_ref[cols, :])
        q_inter = nt(jnp.concatenate([d, d], 1), s_pair)
        k_inter = nt(jnp.concatenate([v, v], 1), jnp.concatenate([after_high, after_low], 1))
        v_inter = nn(jnp.concatenate([k, k], 1), jnp.concatenate([after_high, after_low], 0))
        q_intra0 = nn(p00, k[:HALF])
        q_intra1 = nn(p10, k[:HALF]) + nn(p11, k[HALF:])
        k_intra0 = tn(p00, q0) + tn(p10, q1)
        k_intra1 = tn(p11, q1)
        v_intra0 = tn(a00, d0) + tn(a10, d1)
        v_intra1 = tn(a11, d1)
        qg_ref[:HALF, cols] = (q_intra0 + q_inter[:HALF]).astype(BF16)
        qg_ref[HALF:, cols] = (q_intra1 + q_inter[HALF:]).astype(BF16)
        kg_ref[:HALF, cols] = (k_intra0 + k_inter[:HALF]).astype(BF16)
        kg_ref[HALF:, cols] = (k_intra1 + k_inter[HALF:]).astype(BF16)
        vg_ref[:HALF, cols] = (v_intra0 + v_inter[:HALF]).astype(BF16)
        vg_ref[HALF:, cols] = (v_intra1 + v_inter[HALF:]).astype(BF16)


def params():
    return pltpu.CompilerParams(
        dimension_semantics=("arbitrary",), vmem_limit_bytes=48 * 2**20
    )


def carried_in(value, reverse):
    count = lax.axis_size("ctx")
    rows = value.shape[0] // count
    mine = lax.all_to_all(value.reshape(count, rows, HD), "ctx", 0, 0)
    summed = pl.pallas_call(
        lambda x, o: scan_kernel(reverse, x, o),
        out_shape=jax.ShapeDtypeStruct(mine.shape, F32),
        in_specs=[pl.BlockSpec(memory_space=pltpu.VMEM)],
        out_specs=pl.BlockSpec(memory_space=pltpu.VMEM),
        name="suffix" if reverse else "prefix",
    )(mine)
    return lax.all_to_all(summed, "ctx", 0, 0).reshape(value.shape)


def tp_sum(x):
    n = lax.axis_size("tp")
    for flip in (1, 2, 4):
        x = x + lax.ppermute(x, "tp", [(i, i ^ flip) for i in range(n)])
    return x


def local(queries, keys, values, gate, gain, out_grad):
    rows, width = queries.shape
    steps = width // PAIR
    gain_row = gain.reshape(1, width)
    wide = pl.BlockSpec((rows, PAIR), lambda i: (0, i))
    gain_spec = pl.BlockSpec((1, PAIR), lambda i: (0, i))
    state = pl.BlockSpec((PAIR, HD), lambda i: (i, 0))
    tiles = pl.BlockSpec((2, 3, HALF, HALF), lambda i: (i, 0, 0, 0))
    sums_spec = pl.BlockSpec((2, rows), lambda i: (0, 0))
    half_shape = jax.ShapeDtypeStruct((rows, width), BF16)
    state_shape = jax.ShapeDtypeStruct((width, HD), F32)

    own = pl.pallas_call(
        state_kernel, grid=(steps,), in_specs=[wide, wide], out_specs=state,
        out_shape=state_shape, compiler_params=params(), name="state",
    )(keys, values)
    states = carried_in(own, False)

    mixed, attn, sums = pl.pallas_call(
        forward_kernel,
        grid=(steps,),
        in_specs=[wide, wide, wide, state, wide, gain_spec, wide],
        out_specs=[wide, tiles, sums_spec],
        out_shape=[
            jax.ShapeDtypeStruct((rows, width), F32),
            jax.ShapeDtypeStruct((width // HD, 3, HALF, HALF), BF16),
            jax.ShapeDtypeStruct((2, rows), F32),
        ],
        scratch_shapes=[pltpu.VMEM((rows, HD), F32), pltpu.VMEM((rows, HD), F32)],
        compiler_params=params(), name="forward",
    )(queries, keys, values, states, gate, gain_row, out_grad)
    total = tp_sum(sums)

    output, gate_grad, mixed_grad, own_after = pl.pallas_call(
        norm_kernel,
        grid=(steps,),
        in_specs=[sums_spec, wide, wide, gain_spec, wide, wide],
        out_specs=[wide, wide, wide, state],
        out_shape=[half_shape, half_shape, half_shape, state_shape],
        scratch_shapes=[pltpu.VMEM((rows, HD), F32), pltpu.VMEM((rows, HD), F32)],
        compiler_params=params(), name="norm",
    )(total, mixed, gate, gain_row, out_grad, queries)
    after = carried_in(own_after, True)

    q_grad, k_grad, v_grad = pl.pallas_call(
        backward_kernel,
        grid=(steps,),
        in_specs=[wide, wide, wide, wide, tiles, state, state],
        out_specs=[wide, wide, wide],
        out_shape=[half_shape, half_shape, half_shape],
        compiler_params=params(), name="backward",
    )(queries, keys, values, mixed_grad, attn, states, after)
    return output, q_grad, k_grad, v_grad, gate_grad


def solution(mesh):
    wide = P("ctx", "tp")
    return jax.shard_map(
        local,
        mesh=mesh,
        in_specs=(wide, wide, wide, wide, P("tp"), wide),
        out_specs=(wide, wide, wide, wide, wide),
        check_vma=False,
    )
```

```python
import jax
import jax.numpy as jnp
from jax import lax
from jax.experimental import pallas as pl
from jax.experimental.pallas import tpu as pltpu
from jax.sharding import PartitionSpec as P

HD = 128
D = 8192
EPS = 1e-06
HALF = 256
PAIR = 2 * HD
F32 = jnp.float32
BF16 = jnp.bfloat16


def dot(a, b, dims):
    return lax.dot_general(a, b, (dims, ((), ())), preferred_element_type=F32)


def nn(a, b):
    return dot(a, b, ((1,), (0,)))


def nt(a, b):
    return dot(a, b, ((1,), (1,)))


def tn(a, b):
    return dot(a, b, ((0,), (0,)))


def halves(x):
    high = x.astype(BF16)
    return high, (x - high.astype(F32)).astype(BF16)


def causal_tile(x):
    rows = lax.broadcasted_iota(jnp.int32, x.shape, 0)
    cols = lax.broadcasted_iota(jnp.int32, x.shape, 1)
    return jnp.where(cols <= rows, x, 0.0)


def fetch(source, target, sems, width):
    copies = []
    for i in range(source.shape[1] // width):
        cols = pl.ds(i * width, width)
        copy = pltpu.make_async_copy(source.at[:, cols], target.at[:, cols], sems.at[i])
        copy.start()
        copies.append(copy)
    return copies


def state_kernel(k_ref, v_ref, out_ref, k_buf, v_buf, k_sem, v_sem):
    k_copies = fetch(k_ref, k_buf, k_sem, PAIR)
    v_copies = fetch(v_ref, v_buf, v_sem, PAIR)
    for i in range(len(k_copies)):
        k_copies[i].wait()
        v_copies[i].wait()
        for h in (2 * i, 2 * i + 1):
            cols = slice(h * HD, (h + 1) * HD)
            out_ref[cols, :] = tn(k_buf[:, cols], v_buf[:, cols])


def scan_kernel(reverse, x_ref, out_ref):
    count = x_ref.shape[0]
    running = jnp.zeros(x_ref.shape[1:], F32)
    for step in range(count):
        i = count - 1 - step if reverse else step
        out_ref[i] = running
        running = running + x_ref[i]


def forward_kernel(q_ref, k_ref, v_ref, s_ref, gain_ref, gate_ref, dy_ref,
                   mixed_ref, sums_ref, square, cross):
    heads = q_ref.shape[1] // HD
    for h in range(heads):
        cols = slice(h * HD, (h + 1) * HD)
        q, k, v = q_ref[:, cols], k_ref[:, cols], v_ref[:, cols]
        q0, q1 = q[:HALF], q[HALF:]
        a00 = causal_tile(nt(q0, k[:HALF])).astype(BF16)
        a10 = nt(q1, k[:HALF]).astype(BF16)
        a11 = causal_tile(nt(q1, k[HALF:])).astype(BF16)
        inter = nn(jnp.concatenate([q, q], 1), jnp.concatenate(halves(s_ref[cols, :]), 0))
        mixed_ref[:HALF, cols] = nn(a00, v[:HALF]) + inter[:HALF]
        mixed_ref[HALF:, cols] = nn(a10, v[:HALF]) + nn(a11, v[HALF:]) + inter[HALF:]
    square[...] = jnp.zeros_like(square)
    cross[...] = jnp.zeros_like(cross)
    for h in range(heads):
        cols = slice(h * HD, (h + 1) * HD)
        mixed = mixed_ref[:, cols]
        sig = jax.nn.sigmoid(gate_ref[:, cols].astype(F32))
        dn = dy_ref[:, cols].astype(F32) * gain_ref[:, cols] * sig
        square[...] += mixed * mixed
        cross[...] += dn * mixed
    sums_ref[0:1, :] = jnp.sum(square[...].T, axis=0, keepdims=True)
    sums_ref[1:2, :] = jnp.sum(cross[...].T, axis=0, keepdims=True)


def norm_kernel(sums_ref, mixed_ref, gate_ref, gain_ref, dy_ref, q_ref,
                out_ref, ggrad_ref, d_ref, g_ref,
                out_buf, ggrad_buf, inv_ref, proj_ref, sems):
    total = sums_ref[...]
    inv = lax.rsqrt(total[0:1] / D + EPS)
    proj = inv * (total[1:2] / D)
    inv_ref[...] = jnp.broadcast_to(inv, (HD, inv.shape[1])).T
    proj_ref[...] = jnp.broadcast_to(proj, (HD, proj.shape[1])).T
    copies = []
    for h in range(q_ref.shape[1] // HD):
        cols = slice(h * HD, (h + 1) * HD)
        inv, proj = inv_ref[...], proj_ref[...]
        sig = jax.nn.sigmoid(gate_ref[:, cols].astype(F32))
        gain = gain_ref[:, cols]
        gain_sig = gain * sig
        dn = dy_ref[:, cols].astype(F32) * gain_sig
        normed = mixed_ref[:, cols] * inv
        out_buf[:, cols] = (normed * gain_sig).astype(BF16)
        grad = (inv * (dn - normed * proj)).astype(BF16)
        ggrad_buf[:, cols] = (dn * normed * (1.0 - sig)).astype(BF16)
        d_ref[:, cols] = grad
        g_ref[cols, :] = tn(q_ref[:, cols], grad)
        if h % 2 == 1:
            both = pl.ds((h - 1) * HD, PAIR)
            for j, (buf, ref) in enumerate(((out_buf, out_ref), (ggrad_buf, ggrad_ref))):
                copy = pltpu.make_async_copy(buf.at[:, both], ref.at[:, both], sems.at[j, h // 2])
                copy.start()
                copies.append(copy)
    for copy in copies:
        copy.wait()


def backward_kernel(q_ref, k_ref, v_ref, after_ref, s_ref, d_ref,
                    qg_ref, kg_ref, vg_ref, qg_buf, kg_buf, vg_buf, sems):
    copies = []
    for h in range(q_ref.shape[1] // HD):
        cols = slice(h * HD, (h + 1) * HD)
        q, k, v, d = q_ref[:, cols], k_ref[:, cols], v_ref[:, cols], d_ref[:, cols]
        d0, d1, q0, q1 = d[:HALF], d[HALF:], q[:HALF], q[HALF:]
        p00 = causal_tile(nt(d0, v[:HALF])).astype(BF16)
        p10 = nt(d1, v[:HALF]).astype(BF16)
        p11 = causal_tile(nt(d1, v[HALF:])).astype(BF16)
        a00 = causal_tile(nt(q0, k[:HALF])).astype(BF16)
        a10 = nt(q1, k[:HALF]).astype(BF16)
        a11 = causal_tile(nt(q1, k[HALF:])).astype(BF16)
        after_high, after_low = halves(after_ref[cols, :])
        after_wide = jnp.concatenate([after_high, after_low], 1)
        after_tall = jnp.concatenate([after_high, after_low], 0)
        q_inter = nt(jnp.concatenate([d, d], 1), jnp.concatenate(halves(s_ref[cols, :]), 1))
        k_inter = nt(jnp.concatenate([v, v], 1), after_wide)
        v_inter = nn(jnp.concatenate([k, k], 1), after_tall)
        qg_buf[:HALF, cols] = (nn(p00, k[:HALF]) + q_inter[:HALF]).astype(BF16)
        qg_buf[HALF:, cols] = (nn(p10, k[:HALF]) + nn(p11, k[HALF:]) + q_inter[HALF:]).astype(BF16)
        kg_buf[:HALF, cols] = (tn(p00, q0) + tn(p10, q1) + k_inter[:HALF]).astype(BF16)
        kg_buf[HALF:, cols] = (tn(p11, q1) + k_inter[HALF:]).astype(BF16)
        vg_buf[:HALF, cols] = (tn(a00, d0) + tn(a10, d1) + v_inter[:HALF]).astype(BF16)
        vg_buf[HALF:, cols] = (tn(a11, d1) + v_inter[HALF:]).astype(BF16)
        if h % 2 == 1:
            both = pl.ds((h - 1) * HD, PAIR)
            for j, (buf, ref) in enumerate(((qg_buf, qg_ref), (kg_buf, kg_ref), (vg_buf, vg_ref))):
                copy = pltpu.make_async_copy(buf.at[:, both], ref.at[:, both], sems.at[j, h // 2])
                copy.start()
                copies.append(copy)
    for copy in copies:
        copy.wait()


def params(megabytes):
    return pltpu.CompilerParams(vmem_limit_bytes=megabytes * 2**20)


VM = pl.BlockSpec(memory_space=pltpu.VMEM)
HBM = pl.BlockSpec(memory_space=pltpu.HBM)


def carried_in(value, reverse):
    count = lax.axis_size("ctx")
    rows = value.shape[0] // count
    mine = lax.all_to_all(value.reshape(count, rows, HD), "ctx", 0, 0)
    summed = pl.pallas_call(
        lambda x, o: scan_kernel(reverse, x, o),
        out_shape=jax.ShapeDtypeStruct(mine.shape, F32),
        in_specs=[VM],
        out_specs=VM,
        compiler_params=params(2),
        name="suffix" if reverse else "prefix",
    )(mine)
    return lax.all_to_all(summed, "ctx", 0, 0).reshape(value.shape)


def tp_sum(x):
    n = lax.axis_size("tp")
    x = x + lax.ppermute(x, "tp", [(i, i ^ 1) for i in range(n)])
    others = [lax.ppermute(x, "tp", [(i, i ^ flip) for i in range(n)]) for flip in (4, 2, 6)]
    return x + others[0] + others[1] + others[2]


def local(queries, keys, values, gate, gain, out_grad):
    rows, width = queries.shape
    pairs = width // PAIR
    gain_row = gain.reshape(1, width)
    half_shape = jax.ShapeDtypeStruct((rows, width), BF16)
    state_shape = jax.ShapeDtypeStruct((width, HD), F32)
    half_buf = pltpu.VMEM((rows, width), BF16)
    column = pltpu.VMEM((rows, HD), F32)
    dma = pltpu.SemaphoreType.DMA

    own = pl.pallas_call(
        state_kernel, in_specs=[HBM, HBM], out_specs=VM, out_shape=state_shape,
        scratch_shapes=[half_buf, half_buf, dma((pairs,)), dma((pairs,))],
        compiler_params=params(60), name="state",
    )(keys, values)
    states = carried_in(own, False)

    mixed, sums = pl.pallas_call(
        forward_kernel,
        in_specs=[VM] * 7,
        out_specs=[VM, VM],
        out_shape=[
            jax.ShapeDtypeStruct((rows, width), F32),
            jax.ShapeDtypeStruct((2, rows), F32),
        ],
        scratch_shapes=[column, column],
        compiler_params=params(16), name="forward",
    )(queries, keys, values, states, gain_row, gate, out_grad)
    total = tp_sum(sums)

    output, gate_grad, mixed_grad, own_after = pl.pallas_call(
        norm_kernel,
        in_specs=[VM] * 6,
        out_specs=[HBM, HBM, VM, VM],
        out_shape=[half_shape, half_shape, half_shape, state_shape],
        scratch_shapes=[half_buf, half_buf, column, column, dma((2, pairs))],
        compiler_params=params(16), name="norm",
    )(total, mixed, gate, gain_row, out_grad, queries)
    after = carried_in(own_after, True)

    q_grad, k_grad, v_grad = pl.pallas_call(
        backward_kernel,
        in_specs=[VM] * 6,
        out_specs=[HBM, HBM, HBM],
        out_shape=[half_shape, half_shape, half_shape],
        scratch_shapes=[half_buf, half_buf, half_buf, dma((3, pairs))],
        compiler_params=params(16), name="backward",
    )(queries, keys, values, after, states, mixed_grad)
    return output, q_grad, k_grad, v_grad, gate_grad


def solution(mesh):
    wide = P("ctx", "tp")
    return jax.shard_map(
        local,
        mesh=mesh,
        in_specs=(wide, wide, wide, wide, P("tp"), wide),
        out_specs=(wide, wide, wide, wide, wide),
        check_vma=False,
    )
```

```python
import jax
import jax.numpy as jnp
from jax import lax
from jax.experimental import pallas as pl
from jax.experimental.pallas import tpu as pltpu
from jax.sharding import PartitionSpec as P

HD = 128
D = 8192
EPS = 1e-06
HALF = 256
PAIR = 2 * HD
F32 = jnp.float32
BF16 = jnp.bfloat16


def dot(a, b, dims):
    return lax.dot_general(a, b, (dims, ((), ())), preferred_element_type=F32)


def nn(a, b):
    return dot(a, b, ((1,), (0,)))


def nt(a, b):
    return dot(a, b, ((1,), (1,)))


def tn(a, b):
    return dot(a, b, ((0,), (0,)))


def halves(x):
    high = x.astype(BF16)
    return high, (x - high.astype(F32)).astype(BF16)


def causal_tile(x):
    rows = lax.broadcasted_iota(jnp.int32, x.shape, 0)
    cols = lax.broadcasted_iota(jnp.int32, x.shape, 1)
    return jnp.where(cols <= rows, x, 0.0)


def state_kernel(k_ref, v_ref, out_ref):
    for h in range(k_ref.shape[1] // HD):
        cols = slice(h * HD, (h + 1) * HD)
        out_ref[cols, :] = tn(k_ref[:, cols], v_ref[:, cols])


def scan_kernel(reverse, x_ref, out_ref):
    count = x_ref.shape[0]
    running = jnp.zeros(x_ref.shape[1:], F32)
    for step in range(count):
        i = count - 1 - step if reverse else step
        out_ref[i] = running
        running = running + x_ref[i]


def forward_kernel(q_ref, k_ref, v_ref, s_ref, gain_ref, gate_ref, dy_ref,
                   mixed_ref, sums_ref, square, cross):
    heads = q_ref.shape[1] // HD
    for h in range(heads):
        cols = slice(h * HD, (h + 1) * HD)
        q, k, v = q_ref[:, cols], k_ref[:, cols], v_ref[:, cols]
        q0, q1 = q[:HALF], q[HALF:]
        a00 = causal_tile(nt(q0, k[:HALF])).astype(BF16)
        a10 = nt(q1, k[:HALF]).astype(BF16)
        a11 = causal_tile(nt(q1, k[HALF:])).astype(BF16)
        inter = nn(jnp.concatenate([q, q], 1), jnp.concatenate(halves(s_ref[cols, :]), 0))
        mixed_ref[:HALF, cols] = nn(a00, v[:HALF]) + inter[:HALF]
        mixed_ref[HALF:, cols] = nn(a10, v[:HALF]) + nn(a11, v[HALF:]) + inter[HALF:]
    square[...] = jnp.zeros_like(square)
    cross[...] = jnp.zeros_like(cross)
    for h in range(heads):
        cols = slice(h * HD, (h + 1) * HD)
        mixed = mixed_ref[:, cols]
        sig = jax.nn.sigmoid(gate_ref[:, cols].astype(F32))
        dn = dy_ref[:, cols].astype(F32) * gain_ref[:, cols] * sig
        square[...] += mixed * mixed
        cross[...] += dn * mixed
    sums_ref[0:1, :] = jnp.sum(square[...].T, axis=0, keepdims=True)
    sums_ref[1:2, :] = jnp.sum(cross[...].T, axis=0, keepdims=True)


def norm_kernel(sums0_ref, sums1_ref, sums2_ref, sums3_ref, mixed_ref, gate_ref, gain_ref, dy_ref, q_ref,
                out_ref, ggrad_ref, d_ref, g_ref,
                out_buf, ggrad_buf, inv_ref, proj_ref, sems):
    total = (sums0_ref[...] + sums1_ref[...]) + (sums2_ref[...] + sums3_ref[...])
    inv = lax.rsqrt(total[0:1] / D + EPS)
    proj = inv * (total[1:2] / D)
    inv_ref[...] = jnp.broadcast_to(inv, (HD, inv.shape[1])).T
    proj_ref[...] = jnp.broadcast_to(proj, (HD, proj.shape[1])).T
    copies = []
    for h in range(q_ref.shape[1] // HD):
        cols = slice(h * HD, (h + 1) * HD)
        inv, proj = inv_ref[...], proj_ref[...]
        sig = jax.nn.sigmoid(gate_ref[:, cols].astype(F32))
        gain = gain_ref[:, cols]
        gain_sig = gain * sig
        dn = dy_ref[:, cols].astype(F32) * gain_sig
        normed = mixed_ref[:, cols] * inv
        out_buf[:, cols] = (normed * gain_sig).astype(BF16)
        grad = (inv * (dn - normed * proj)).astype(BF16)
        ggrad_buf[:, cols] = (dn * normed * (1.0 - sig)).astype(BF16)
        d_ref[:, cols] = grad
        g_ref[cols, :] = tn(q_ref[:, cols], grad)
        if h % 2 == 1:
            both = pl.ds((h - 1) * HD, PAIR)
            for j, (buf, ref) in enumerate(((out_buf, out_ref), (ggrad_buf, ggrad_ref))):
                copy = pltpu.make_async_copy(buf.at[:, both], ref.at[:, both], sems.at[j, h // 2])
                copy.start()
                copies.append(copy)
    for copy in copies:
        copy.wait()


def partial_kernel(q_ref, k_ref, v_ref, s_ref, d_ref, qg_ref, parts_ref, qg_buf, sems):
    rows = q_ref.shape[0]
    copies = []
    for h in range(q_ref.shape[1] // HD):
        cols = slice(h * HD, (h + 1) * HD)
        q, k, v, d = q_ref[:, cols], k_ref[:, cols], v_ref[:, cols], d_ref[:, cols]
        d0, d1, q0, q1 = d[:HALF], d[HALF:], q[:HALF], q[HALF:]
        p00 = causal_tile(nt(d0, v[:HALF])).astype(BF16)
        p10 = nt(d1, v[:HALF]).astype(BF16)
        p11 = causal_tile(nt(d1, v[HALF:])).astype(BF16)
        a00 = causal_tile(nt(q0, k[:HALF])).astype(BF16)
        a10 = nt(q1, k[:HALF]).astype(BF16)
        a11 = causal_tile(nt(q1, k[HALF:])).astype(BF16)
        q_inter = nt(jnp.concatenate([d, d], 1), jnp.concatenate(halves(s_ref[cols, :]), 1))
        qg_buf[:HALF, cols] = (nn(p00, k[:HALF]) + q_inter[:HALF]).astype(BF16)
        qg_buf[HALF:, cols] = (nn(p10, k[:HALF]) + nn(p11, k[HALF:]) + q_inter[HALF:]).astype(BF16)
        parts_ref[:HALF, cols] = (tn(p00, q0) + tn(p10, q1)).astype(BF16)
        parts_ref[HALF:rows, cols] = (tn(p11, q1)).astype(BF16)
        parts_ref[rows : rows + HALF, cols] = (tn(a00, d0) + tn(a10, d1)).astype(BF16)
        parts_ref[rows + HALF :, cols] = (tn(a11, d1)).astype(BF16)
        if h % 2 == 1:
            both = pl.ds((h - 1) * HD, PAIR)
            copy = pltpu.make_async_copy(qg_buf.at[:, both], qg_ref.at[:, both], sems.at[h // 2])
            copy.start()
            copies.append(copy)
    for copy in copies:
        copy.wait()


def gradient_kernel(k_ref, v_ref, after_ref, parts_ref, kg_ref, vg_ref, kg_buf, vg_buf, sems):
    rows = k_ref.shape[0]
    copies = []
    for h in range(k_ref.shape[1] // HD):
        cols = slice(h * HD, (h + 1) * HD)
        k, v = k_ref[:, cols], v_ref[:, cols]
        after_high, after_low = halves(after_ref[cols, :])
        k_inter = nt(jnp.concatenate([v, v], 1), jnp.concatenate([after_high, after_low], 1))
        v_inter = nn(jnp.concatenate([k, k], 1), jnp.concatenate([after_high, after_low], 0))
        kg_buf[:, cols] = (parts_ref[:rows, cols] + k_inter).astype(BF16)
        vg_buf[:, cols] = (parts_ref[rows:, cols] + v_inter).astype(BF16)
        if h % 2 == 1:
            both = pl.ds((h - 1) * HD, PAIR)
            for j, (buf, ref) in enumerate(((kg_buf, kg_ref), (vg_buf, vg_ref))):
                copy = pltpu.make_async_copy(buf.at[:, both], ref.at[:, both], sems.at[j, h // 2])
                copy.start()
                copies.append(copy)
    for copy in copies:
        copy.wait()


def cost(flops, moved):
    return pl.CostEstimate(flops=flops, bytes_accessed=moved, transcendentals=0)


def params(megabytes):
    return pltpu.CompilerParams(vmem_limit_bytes=megabytes * 2**20)


VM = pl.BlockSpec(memory_space=pltpu.VMEM)
HBM = pl.BlockSpec(memory_space=pltpu.HBM)


def carried_in(value, reverse):
    count = lax.axis_size("ctx")
    rows = value.shape[0] // count
    mine = lax.all_to_all(value.reshape(count, rows, HD), "ctx", 0, 0)
    summed = pl.pallas_call(
        lambda x, o: scan_kernel(reverse, x, o),
        out_shape=jax.ShapeDtypeStruct(mine.shape, F32),
        in_specs=[VM],
        out_specs=VM,
        compiler_params=params(2),
        name="suffix" if reverse else "prefix",
    )(mine)
    return lax.all_to_all(summed, "ctx", 0, 0).reshape(value.shape)


def tp_parts(x):
    n = lax.axis_size("tp")
    x = x + lax.ppermute(x, "tp", [(i, i ^ 1) for i in range(n)])
    return [x] + [lax.ppermute(x, "tp", [(i, i ^ flip) for i in range(n)]) for flip in (4, 2, 6)]


def local(queries, keys, values, gate, gain, out_grad):
    rows, width = queries.shape
    pairs = width // PAIR
    gain_row = gain.reshape(1, width)
    half_shape = jax.ShapeDtypeStruct((rows, width), BF16)
    double_shape = jax.ShapeDtypeStruct((2 * rows, width), BF16)
    state_shape = jax.ShapeDtypeStruct((width, HD), F32)
    half_buf = pltpu.VMEM((rows, width), BF16)
    column = pltpu.VMEM((rows, HD), F32)
    dma = pltpu.SemaphoreType.DMA

    own = pl.pallas_call(
        state_kernel, in_specs=[VM, VM], out_specs=VM, out_shape=state_shape,
        compiler_params=params(8), name="state",
    )(keys, values)
    states = carried_in(own, False)

    mixed, sums = pl.pallas_call(
        forward_kernel,
        in_specs=[VM] * 7,
        out_specs=[VM, VM],
        out_shape=[
            jax.ShapeDtypeStruct((rows, width), F32),
            jax.ShapeDtypeStruct((2, rows), F32),
        ],
        scratch_shapes=[column, column],
        compiler_params=params(16), name="forward",
    )(queries, keys, values, states, gain_row, gate, out_grad)

    output, gate_grad, mixed_grad, own_after = pl.pallas_call(
        norm_kernel,
        in_specs=[VM] * 9,
        out_specs=[HBM, HBM, VM, VM],
        out_shape=[half_shape, half_shape, half_shape, state_shape],
        scratch_shapes=[half_buf, half_buf, column, column, dma((2, pairs))],
        compiler_params=params(16), name="norm",
    )(*tp_parts(sums), mixed, gate, gain_row, out_grad, queries)
    after = carried_in(own_after, True)

    q_grad, parts = pl.pallas_call(
        partial_kernel,
        in_specs=[VM] * 5,
        out_specs=[HBM, VM],
        out_shape=[half_shape, double_shape],
        scratch_shapes=[half_buf, dma((pairs,))],
        compiler_params=params(16), cost_estimate=cost(5 * 10**9, 10 * 2**20), name="partial",
    )(queries, keys, values, states, mixed_grad)
    k_grad, v_grad = pl.pallas_call(
        gradient_kernel,
        in_specs=[VM] * 4,
        out_specs=[HBM, HBM],
        out_shape=[half_shape, half_shape],
        scratch_shapes=[half_buf, half_buf, dma((2, pairs))],
        compiler_params=params(16), name="gradient",
    )(keys, values, after, parts)
    return output, q_grad, k_grad, v_grad, gate_grad


def solution(mesh):
    wide = P("ctx", "tp")
    return jax.shard_map(
        local,
        mesh=mesh,
        in_specs=(wide, wide, wide, wide, P("tp"), wide),
        out_specs=(wide, wide, wide, wide, wide),
        check_vma=False,
    )
```

```python
import jax
import jax.numpy as jnp
from jax import lax
from jax.experimental import pallas as pl
from jax.experimental.pallas import tpu as pltpu
from jax.sharding import PartitionSpec as P

HD = 128
D = 8192
EPS = 1e-06
HALF = 256
PAIR = 2 * HD
F32 = jnp.float32
BF16 = jnp.bfloat16


def dot(a, b, dims):
    return lax.dot_general(a, b, (dims, ((), ())), preferred_element_type=F32)


def nn(a, b):
    return dot(a, b, ((1,), (0,)))


def nt(a, b):
    return dot(a, b, ((1,), (1,)))


def tn(a, b):
    return dot(a, b, ((0,), (0,)))


def halves(x):
    high = x.astype(BF16)
    return high, (x - high.astype(F32)).astype(BF16)


def causal_tile(x):
    rows = lax.broadcasted_iota(jnp.int32, x.shape, 0)
    cols = lax.broadcasted_iota(jnp.int32, x.shape, 1)
    return jnp.where(cols <= rows, x, 0.0)


def state_kernel(k_ref, v_ref, out_ref):
    for h in range(k_ref.shape[1] // HD):
        cols = slice(h * HD, (h + 1) * HD)
        out_ref[cols, :] = tn(k_ref[:, cols], v_ref[:, cols])


def scan_kernel(reverse, x_ref, out_ref):
    count = x_ref.shape[0]
    running = jnp.zeros(x_ref.shape[1:], F32)
    for step in range(count):
        i = count - 1 - step if reverse else step
        out_ref[i] = running
        running = running + x_ref[i]


def forward_kernel(q_ref, k_ref, v_ref, s_ref, gain_ref, gate_ref, dy_ref,
                   mixed_ref, sums_ref, square, cross):
    heads = q_ref.shape[1] // HD
    for h in range(heads):
        cols = slice(h * HD, (h + 1) * HD)
        q, k, v = q_ref[:, cols], k_ref[:, cols], v_ref[:, cols]
        q0, q1 = q[:HALF], q[HALF:]
        a00 = causal_tile(nt(q0, k[:HALF])).astype(BF16)
        a10 = nt(q1, k[:HALF]).astype(BF16)
        a11 = causal_tile(nt(q1, k[HALF:])).astype(BF16)
        inter = nn(jnp.concatenate([q, q], 1), jnp.concatenate(halves(s_ref[cols, :]), 0))
        mixed_ref[:HALF, cols] = nn(a00, v[:HALF]) + inter[:HALF]
        mixed_ref[HALF:, cols] = nn(a10, v[:HALF]) + nn(a11, v[HALF:]) + inter[HALF:]
    square[...] = jnp.zeros_like(square)
    cross[...] = jnp.zeros_like(cross)
    for h in range(heads):
        cols = slice(h * HD, (h + 1) * HD)
        mixed = mixed_ref[:, cols]
        sig = jax.nn.sigmoid(gate_ref[:, cols].astype(F32))
        dn = dy_ref[:, cols].astype(F32) * gain_ref[:, cols] * sig
        square[...] += mixed * mixed
        cross[...] += dn * mixed
    sums_ref[0:1, :] = jnp.sum(square[...].T, axis=0, keepdims=True)
    sums_ref[1:2, :] = jnp.sum(cross[...].T, axis=0, keepdims=True)


def norm_kernel(sums0_ref, sums1_ref, sums2_ref, sums3_ref, mixed_ref, gate_ref, gain_ref, dy_ref, q_ref,
                d_ref, g_ref, inv_ref, proj_ref):
    total = (sums0_ref[...] + sums1_ref[...]) + (sums2_ref[...] + sums3_ref[...])
    inv = lax.rsqrt(total[0:1] / D + EPS)
    proj = inv * (total[1:2] / D)
    inv_ref[...] = jnp.broadcast_to(inv, (HD, inv.shape[1])).T
    proj_ref[...] = jnp.broadcast_to(proj, (HD, proj.shape[1])).T
    for h in range(q_ref.shape[1] // HD):
        cols = slice(h * HD, (h + 1) * HD)
        inv = inv_ref[...]
        sig = jax.nn.sigmoid(gate_ref[:, cols].astype(F32))
        dn = dy_ref[:, cols].astype(F32) * (gain_ref[:, cols] * sig)
        normed = mixed_ref[:, cols] * inv
        grad = (inv * (dn - normed * proj_ref[...])).astype(BF16)
        d_ref[:, cols] = grad
        g_ref[cols, :] = tn(q_ref[:, cols], grad)


def output_kernel(mixed_ref, inv_ref, gate_ref, gain_ref, dy_ref, out_ref, ggrad_ref, out_buf, ggrad_buf, sems):
    copies = []
    for h in range(mixed_ref.shape[1] // HD):
        cols = slice(h * HD, (h + 1) * HD)
        normed = mixed_ref[:, cols] * inv_ref[...]
        sig = jax.nn.sigmoid(gate_ref[:, cols].astype(F32))
        scale = gain_ref[:, cols] * sig
        dn = dy_ref[:, cols].astype(F32) * scale
        out_buf[:, cols] = (normed * scale).astype(BF16)
        ggrad_buf[:, cols] = (dn * normed * (1.0 - sig)).astype(BF16)
        if h % 2 == 1:
            both = pl.ds((h - 1) * HD, PAIR)
            for j, (buf, ref) in enumerate(((out_buf, out_ref), (ggrad_buf, ggrad_ref))):
                copy = pltpu.make_async_copy(buf.at[:, both], ref.at[:, both], sems.at[j, h // 2])
                copy.start()
                copies.append(copy)
    for copy in copies:
        copy.wait()


def partial_kernel(q_ref, k_ref, v_ref, s_ref, d_ref, qg_ref, parts_ref, qg_buf, sems):
    rows = q_ref.shape[0]
    copies = []
    for h in range(q_ref.shape[1] // HD):
        cols = slice(h * HD, (h + 1) * HD)
        q, k, v, d = q_ref[:, cols], k_ref[:, cols], v_ref[:, cols], d_ref[:, cols]
        d0, d1, q0, q1 = d[:HALF], d[HALF:], q[:HALF], q[HALF:]
        p00 = causal_tile(nt(d0, v[:HALF])).astype(BF16)
        p10 = nt(d1, v[:HALF]).astype(BF16)
        p11 = causal_tile(nt(d1, v[HALF:])).astype(BF16)
        a00 = causal_tile(nt(q0, k[:HALF])).astype(BF16)
        a10 = nt(q1, k[:HALF]).astype(BF16)
        a11 = causal_tile(nt(q1, k[HALF:])).astype(BF16)
        q_inter = nt(jnp.concatenate([d, d], 1), jnp.concatenate(halves(s_ref[cols, :]), 1))
        qg_buf[:HALF, cols] = (nn(p00, k[:HALF]) + q_inter[:HALF]).astype(BF16)
        qg_buf[HALF:, cols] = (nn(p10, k[:HALF]) + nn(p11, k[HALF:]) + q_inter[HALF:]).astype(BF16)
        parts_ref[:HALF, cols] = (tn(p00, q0) + tn(p10, q1)).astype(BF16)
        parts_ref[HALF:rows, cols] = (tn(p11, q1)).astype(BF16)
        parts_ref[rows : rows + HALF, cols] = (tn(a00, d0) + tn(a10, d1)).astype(BF16)
        parts_ref[rows + HALF :, cols] = (tn(a11, d1)).astype(BF16)
        if h % 2 == 1:
            both = pl.ds((h - 1) * HD, PAIR)
            copy = pltpu.make_async_copy(qg_buf.at[:, both], qg_ref.at[:, both], sems.at[h // 2])
            copy.start()
            copies.append(copy)
    for copy in copies:
        copy.wait()


def gradient_kernel(k_ref, v_ref, after_ref, parts_ref, kg_ref, vg_ref, kg_buf, vg_buf, sems):
    rows = k_ref.shape[0]
    copies = []
    for h in range(k_ref.shape[1] // HD):
        cols = slice(h * HD, (h + 1) * HD)
        k, v = k_ref[:, cols], v_ref[:, cols]
        after_high, after_low = halves(after_ref[cols, :])
        k_inter = nt(jnp.concatenate([v, v], 1), jnp.concatenate([after_high, after_low], 1))
        v_inter = nn(jnp.concatenate([k, k], 1), jnp.concatenate([after_high, after_low], 0))
        kg_buf[:, cols] = (parts_ref[:rows, cols] + k_inter).astype(BF16)
        vg_buf[:, cols] = (parts_ref[rows:, cols] + v_inter).astype(BF16)
        if h % 2 == 1:
            both = pl.ds((h - 1) * HD, PAIR)
            for j, (buf, ref) in enumerate(((kg_buf, kg_ref), (vg_buf, vg_ref))):
                copy = pltpu.make_async_copy(buf.at[:, both], ref.at[:, both], sems.at[j, h // 2])
                copy.start()
                copies.append(copy)
    for copy in copies:
        copy.wait()


def cost(flops, moved):
    return pl.CostEstimate(flops=flops, bytes_accessed=moved, transcendentals=0)


def params(megabytes):
    return pltpu.CompilerParams(vmem_limit_bytes=megabytes * 2**20)


VM = pl.BlockSpec(memory_space=pltpu.VMEM)
HBM = pl.BlockSpec(memory_space=pltpu.HBM)


def carried_in(value, reverse):
    count = lax.axis_size("ctx")
    rows = value.shape[0] // count
    mine = lax.all_to_all(value.reshape(count, rows, HD), "ctx", 0, 0)
    summed = pl.pallas_call(
        lambda x, o: scan_kernel(reverse, x, o),
        out_shape=jax.ShapeDtypeStruct(mine.shape, F32),
        in_specs=[VM],
        out_specs=VM,
        compiler_params=params(2),
        name="suffix" if reverse else "prefix",
    )(mine)
    return lax.all_to_all(summed, "ctx", 0, 0).reshape(value.shape)


def tp_parts(x):
    n = lax.axis_size("tp")
    x = x + lax.ppermute(x, "tp", [(i, i ^ 1) for i in range(n)])
    return [x] + [lax.ppermute(x, "tp", [(i, i ^ flip) for i in range(n)]) for flip in (4, 2, 6)]


def local(queries, keys, values, gate, gain, out_grad):
    rows, width = queries.shape
    pairs = width // PAIR
    gain_row = gain.reshape(1, width)
    half_shape = jax.ShapeDtypeStruct((rows, width), BF16)
    double_shape = jax.ShapeDtypeStruct((2 * rows, width), BF16)
    state_shape = jax.ShapeDtypeStruct((width, HD), F32)
    half_buf = pltpu.VMEM((rows, width), BF16)
    column = pltpu.VMEM((rows, HD), F32)
    dma = pltpu.SemaphoreType.DMA

    own = pl.pallas_call(
        state_kernel, in_specs=[VM, VM], out_specs=VM, out_shape=state_shape,
        compiler_params=params(8), name="state",
    )(keys, values)
    states = carried_in(own, False)

    mixed, sums = pl.pallas_call(
        forward_kernel,
        in_specs=[VM] * 7,
        out_specs=[VM, VM],
        out_shape=[
            jax.ShapeDtypeStruct((rows, width), F32),
            jax.ShapeDtypeStruct((2, rows), F32),
        ],
        scratch_shapes=[column, column],
        compiler_params=params(16), name="forward",
    )(queries, keys, values, states, gain_row, gate, out_grad)

    mixed_grad, own_after, inv = pl.pallas_call(
        norm_kernel,
        in_specs=[VM] * 9,
        out_specs=[VM, VM, VM],
        out_shape=[half_shape, state_shape, jax.ShapeDtypeStruct((rows, HD), F32)],
        scratch_shapes=[column],
        compiler_params=params(12), name="norm",
    )(*tp_parts(sums), mixed, gate, gain_row, out_grad, queries)

    output, gate_grad = pl.pallas_call(
        output_kernel,
        in_specs=[VM] * 5,
        out_specs=[HBM, HBM],
        out_shape=[half_shape, half_shape],
        scratch_shapes=[half_buf, half_buf, dma((2, pairs))],
        compiler_params=params(12), cost_estimate=cost(10**9, 8 * 2**20), name="output",
    )(mixed, inv, gate, gain_row, out_grad)

    after = carried_in(own_after, True)

    q_grad, parts = pl.pallas_call(
        partial_kernel,
        in_specs=[VM] * 5,
        out_specs=[HBM, VM],
        out_shape=[half_shape, double_shape],
        scratch_shapes=[half_buf, dma((pairs,))],
        compiler_params=params(16), cost_estimate=cost(5 * 10**9, 10 * 2**20), name="partial",
    )(queries, keys, values, states, mixed_grad)
    k_grad, v_grad = pl.pallas_call(
        gradient_kernel,
        in_specs=[VM] * 4,
        out_specs=[HBM, HBM],
        out_shape=[half_shape, half_shape],
        scratch_shapes=[half_buf, half_buf, dma((2, pairs))],
        compiler_params=params(16), name="gradient",
    )(keys, values, after, parts)
    return output, q_grad, k_grad, v_grad, gate_grad


def solution(mesh):
    wide = P("ctx", "tp")
    return jax.shard_map(
        local,
        mesh=mesh,
        in_specs=(wide, wide, wide, wide, P("tp"), wide),
        out_specs=(wide, wide, wide, wide, wide),
        check_vma=False,
    )
```
